32 devices in a mesh: seg: 4 (over y, core), term: 8 (over z, x).
Axes of the slice: x: 2, y: 2, z: 4, core: 2. Of those that a mesh axis runs over, the one named last changes fastest.
Arguments:
- envs_left: float32 [4, 16, 8, 128, 128], P('seg', 'term'), may hold values from -0.5 to 0.5
- envs_right: float32 [4, 16, 8, 128, 128], P('seg', 'term'), may hold values from -0.5 to 0.5
- site_left: float32 [4, 6, 128, 128], P('seg'), may hold values from -6 to 6
- site_right: float32 [4, 6, 128, 128], P('seg'), may hold values from -6 to 6
- precondition: float32 [4, 6, 16384], P('seg'), may hold values from 1 to 10
- source_block: int32 [4, 16, 6], P('seg', 'term'), may hold values from -1 to 5, as said below
- left_tile: int32 [4, 6], P('seg'), may hold values from 0 to 7
- right_tile: int32 [4, 6], P('seg'), may hold values from 0 to 7
Outputs:
- ground_vector: float32 [4, 6, 16384], P('seg', None, 'term')
- ground_energy: float32 [4], P('seg')
The draws below stay inside these ranges and needn't reach their ends.
Inputs may be any that keep to these rules, and one draw needn't show every extreme that they name: `source_block`: -1 means that the term leaves the output block out; every term's non-negative entries are distinct blocks, and the number of blocks a term feeds varies from 1 to 6 over the terms.
All inputs are finite; a program needn't handle non-finite values.
Results may differ from the reference program's by a relative error of at most 0.0003.
Values sent between devices are 32-bit elements; how exact they have to be, the bound alone decides.
A program may use at most 64 MiB of HBM per device.

```python
import math
import jax
import jax.numpy as jnp
from jax import lax

TILE = 128
NT = 8
NBLK = 6
ITERS = 4
TERMS = 16
SEGS = 4


def draw_source_block(key, part):
    key = jax.random.fold_in(key, 7)
    order_key, rank_key, count_key = jax.random.split(key, 3)
    grid_shape = (SEGS, TERMS, NBLK)
    block_ramp = jnp.arange(NBLK, dtype=jnp.int32)
    order_values = jax.random.randint(order_key, grid_shape, 0, 1 << 20, dtype=jnp.int32) * NBLK + block_ramp
    sources = jnp.argsort(order_values, axis=-1).astype(jnp.int32)
    rank_values = jax.random.randint(rank_key, grid_shape, 0, 1 << 20, dtype=jnp.int32) * NBLK + block_ramp
    rank_order = jnp.argsort(jnp.argsort(rank_values, axis=-1), axis=-1).astype(jnp.int32)
    counts = jax.random.randint(count_key, (SEGS, TERMS, 1), 1, NBLK + 1, dtype=jnp.int32)
    term_ids = jnp.arange(TERMS, dtype=jnp.int32)[None, :, None]
    counts = jnp.where(term_ids == 0, NBLK, jnp.where(term_ids == 1, 1, counts))
    return jnp.where(rank_order < counts, sources, -1).astype(jnp.int32)


def touch_ends(drawn, own_key, least, largest):
    longest = drawn.shape.index(max(drawn.shape))
    spots = []
    for shift in (0, 1):
        where = [jax.random.randint(jax.random.fold_in(own_key, axis), (), 0, length) for axis, length in enumerate(drawn.shape)]
        where[longest] = (where[longest] + shift) % drawn.shape[longest]
        spots.append(tuple(where))
    return drawn.at[spots[0]].set(least).at[spots[1]].set(largest)


def levels(rng, shape, cuts, low, top_value):
    def one(axis_at, blocks):
        draws = jax.random.uniform(jax.random.fold_in(jax.random.fold_in(rng, 6), axis_at), (blocks,), jnp.float32, low / len(cuts), top_value / len(cuts))
        return jnp.repeat(jnp.exp(draws), shape[axis_at] // blocks).reshape((-1,) + (1,) * (len(shape) - axis_at - 1))

    factor_of = one(*cuts[0])
    for cut in cuts[1:]:
        factor_of = factor_of * one(*cut)
    return factor_of


def gaussian(rng, extent, scale, limit, cuts=(), kind=jnp.bfloat16):
    array = jax.random.normal(rng, extent, jnp.float32) * scale
    if len(cuts) > 0:
        array = levels(rng, extent, cuts, -0.22, 0.18) * array
    return jnp.clip(array, min=-limit, max=limit).astype(kind)


def setup_inputs(seed: int = 0) -> dict:
    splits = jax.random.split(jax.random.key(seed), 9)
    return {
        "envs_left": gaussian(splits[0], (SEGS, TERMS, NT, TILE, TILE), TILE ** -0.5, 0.5, ((0, 4), (1, 8)), jnp.float32),
        "envs_right": gaussian(splits[1], (SEGS, TERMS, NT, TILE, TILE), TILE ** -0.5, 0.5, ((0, 4), (1, 8)), jnp.float32),
        "site_left": gaussian(splits[2], (SEGS, NBLK, TILE, TILE), 1.0, 6.0, ((0, 4),), jnp.float32),
        "site_right": gaussian(splits[3], (SEGS, NBLK, TILE, TILE), 1.0, 6.0, ((0, 4),), jnp.float32),
        "precondition": jnp.clip(jnp.exp(math.log(10.0) - 2.3025851 * jax.random.uniform(splits[4], (SEGS, NBLK, TILE * TILE), jnp.float32) ** levels(splits[4], (SEGS, NBLK, TILE * TILE), ((0, 4),), -0.2, 0.2)), 1.0, 10.0),
        "source_block": draw_source_block(jax.random.fold_in(splits[8], 71), 0),
        "left_tile": touch_ends(jax.random.randint(splits[6], (SEGS, NBLK), 0, NT), jax.random.fold_in(splits[6], 1), 0, NT - 1).astype(jnp.int32),
        "right_tile": touch_ends(jax.random.randint(splits[7], (SEGS, NBLK), 0, NT), jax.random.fold_in(splits[7], 1), 0, NT - 1).astype(jnp.int32),
    }


FINEST = lax.Precision.HIGHEST
EPSILON = 1e-06

def apply_terms(vector, left_envs, right_envs, sources, left_ids, right_ids):
    tile_stack = vector.reshape(NBLK, TILE, TILE)

    def add_term(summed, member):
        left_env, right_env, source_row = member
        pieces = tile_stack[jnp.clip(source_row, 0, NBLK - 1).astype(jnp.int32)]
        inner_prod = jnp.einsum('kab,kbc->kac', left_env[left_ids], pieces, precision=FINEST)
        outer_prod = jnp.einsum('kac,kdc->kad', inner_prod, right_env[right_ids], precision=FINEST)
        active_mask = (source_row >= 0)[:, None, None]
        return (summed + jnp.where(active_mask, outer_prod, jnp.zeros_like(outer_prod)), None)
    summed, unused = lax.scan(add_term, jnp.zeros((NBLK, TILE, TILE), jnp.float32), (left_envs, right_envs, sources))
    return summed.reshape(NBLK, TILE * TILE)

def ritz_pair(energy, coupling, curvature):
    half_gap = 0.5 * (energy - curvature)
    radius = jnp.sqrt(half_gap * half_gap + coupling * coupling)
    lowest = 0.5 * (energy + curvature) - radius
    keep_coef = jnp.where(half_gap >= 0, coupling * coupling / (radius + jnp.abs(half_gap)), radius - half_gap)
    length = jnp.sqrt(keep_coef * keep_coef + coupling * coupling)
    return (lowest, keep_coef / length, -coupling / length)

def solve_boundary(member):
    left_envs, right_envs, site_a, site_b, precond, sources, left_ids, right_ids = member
    guess = jnp.einsum('kab,kbc->kac', site_a, site_b, precision=FINEST).reshape(NBLK, TILE * TILE)
    vector = guess / jnp.sqrt(jnp.sum(guess * guess) + EPSILON)
    image = apply_terms(vector, left_envs, right_envs, sources, left_ids, right_ids)
    for iteration in range(ITERS):
        energy = jnp.sum(vector * image)
        residual = image - energy * vector
        scaled = residual / precond
        projection = jnp.sum(vector * scaled)
        remainder = scaled - projection * vector
        search = remainder / jnp.sqrt(jnp.sum(remainder * remainder) + EPSILON)
        search_image = apply_terms(search, left_envs, right_envs, sources, left_ids, right_ids)
        coupling = 0.5 * (jnp.sum(vector * search_image) + jnp.sum(search * image))
        curvature = jnp.sum(search * search_image)
        lowest, keep_coef, mix_coef = ritz_pair(energy, coupling, curvature)
        vector = keep_coef * vector + mix_coef * search
        image = keep_coef * image + mix_coef * search_image
    energy = jnp.sum(vector * image)
    return (vector * math.sqrt(NBLK * TILE * TILE), energy)

def reference(envs_left, envs_right, site_left, site_right, precondition, source_block, left_tile, right_tile):
    envs_next = jnp.roll(envs_right, -1, axis=0)
    site_next = jnp.roll(site_right, -1, axis=0)
    vectors, energies = lax.map(solve_boundary, (envs_left, envs_next, site_left, site_next, precondition, source_block, left_tile, right_tile))
    return (vectors, energies)
```

```python
import functools
import math

import jax
import jax.numpy as jnp
from jax import lax
from jax.experimental import pallas as pl
from jax.experimental.pallas import tpu as pltpu
from jax.sharding import PartitionSpec as P

ITERS = 4
EPSILON = 1e-06
MESH = pl.DeviceIdType.MESH
F32 = jnp.float32
BF16 = jnp.bfloat16


def split(value):
    high = value.astype(BF16)
    low = (value - high.astype(F32)).astype(BF16)
    return high, low


def dot(a, b):
    return lax.dot_general(a, b, (((1,), (0,)), ((), ())), preferred_element_type=F32)


def total_of(value):
    return jnp.sum(jnp.sum(value, axis=0, keepdims=True), axis=1, keepdims=True)


def folded(value):
    return jnp.sum(value.reshape(value.shape[0] // 8, 8, value.shape[1]), axis=0)


def kernel(
    devices, segs, blocks, tile, terms, share,
    left_hbm, right_hbm, site_left_hbm, site_right_hbm, precond_hbm, sources, left_ids, right_ids,
    out_ref, energy_ref,
    left, right, site_left, site_right, precond, left_split, right_high, right_low,
    search_high, search_low, picked, feed_high, feed_low, inverse, search, vector, image, search_image, part, pair_in, line_out, line_in,
    local_sems, seg_send, seg_recv, pair_send, pair_recv, line_send, line_recv,
    out_send, out_recv, across_send, across_recv,
):
    me = lax.axis_index("term")
    seg = lax.axis_index("seg")
    column, place = me % 2, me // 2
    places = devices // 2
    partner = place * 2 + 1 - column
    before, after = (seg + segs - 1) % segs, (seg + 1) % segs
    piece = blocks * tile // devices

    def rows(owner):
        return pl.ds(pl.multiple_of(owner * piece, 8), piece)

    def peer(distance):
        return (place + distance) % places

    locals_ = [
        pltpu.make_async_copy(source, target, local_sems.at[n])
        for n, (source, target) in enumerate(
            [(site_left_hbm, site_left), (left_hbm, left), (precond_hbm, precond)]
        )
    ]
    for copy in locals_:
        copy.start()

    barrier = pltpu.get_barrier_semaphore()
    pl.semaphore_signal(barrier, inc=1, device_id={"seg": before}, device_id_type=MESH)
    pl.semaphore_signal(barrier, inc=1, device_id={"seg": after}, device_id_type=MESH)
    pl.semaphore_signal(barrier, inc=1, device_id={"term": partner}, device_id_type=MESH)
    for distance in range(1, places):
        pl.semaphore_signal(
            barrier, inc=1, device_id={"term": peer(distance) * 2 + column}, device_id_type=MESH
        )
    pl.semaphore_wait(barrier, places + 2)

    seg_copies = [
        pltpu.make_async_remote_copy(
            src_ref=source, dst_ref=target, send_sem=seg_send.at[n], recv_sem=seg_recv.at[n],
            device_id={"seg": before}, device_id_type=MESH,
        )
        for n, (source, target) in enumerate([(site_right_hbm, site_right), (right_hbm, right)])
    ]
    for copy in seg_copies:
        copy.start()

    locals_[1].wait()
    def pick_left(k, carry):
        for t in range(terms):
            picked[t * blocks + k] = left[t, left_ids[k]] * (sources[t, k] >= 0).astype(F32)
        return carry

    lax.fori_loop(0, blocks, pick_left, 0)

    def split_left(n, carry):
        high, low = split(picked[n])
        left_split[n, :tile] = high
        left_split[n, tile:] = low
        return carry

    lax.fori_loop(0, terms * blocks, split_left, 0)
    locals_[2].wait()
    for k in range(blocks):
        inverse[k * tile:(k + 1) * tile] = 1.0 / precond[k:k + 1, :].reshape(tile, tile)
    vector[...] = jnp.zeros_like(vector)
    image[...] = jnp.zeros_like(image)

    zero = jnp.zeros((8, tile), F32)

    def at(k):
        return pl.ds(pl.multiple_of(k * tile, tile), tile)

    def store_search(length):
        def block(k, carry):
            value = search[at(k)] * length
            search[at(k)] = value
            high, low = split(value)
            search_high[k] = high
            search_low[k] = low
            return carry

        lax.fori_loop(0, blocks, block, 0)

    locals_[0].wait()
    seg_copies[0].wait()
    def guess(k, total):
        a_high, a_low = split(site_left[k])
        b_high, b_low = split(site_right[k])
        value = dot(a_high, b_high) + (dot(a_high, b_low) + dot(a_low, b_high))
        search[at(k)] = value
        return total + folded(value * value)

    store_search(1.0 / jnp.sqrt(total_of(lax.fori_loop(0, blocks, guess, zero)) + EPSILON))

    seg_copies[1].wait()
    def pick_right(k, carry):
        for t in range(terms):
            picked[t * blocks + k] = right[t, right_ids[k]]
        return carry

    lax.fori_loop(0, blocks, pick_right, 0)

    def split_right(k, carry):
        for t in range(terms):
            high, low = split(picked[t * blocks + k].T)
            right_high[k, t * tile:(t + 1) * tile] = high
            right_low[k, t * tile:(t + 1) * tile] = low
        return carry

    lax.fori_loop(0, blocks, split_right, 0)

    def apply_local():
        def pick(k, carry):
            for t in range(terms):
                source = jnp.maximum(sources[t, k], 0)
                feed_high[t * blocks + k] = search_high[source]
                feed_low[t * blocks + k] = search_low[source]
            return carry

        lax.fori_loop(0, blocks, pick, 0)

        def block(k, carry):
            highs, lows = [], []
            for t in range(terms):
                held = t * blocks + k
                both = dot(left_split[held], feed_high[held])
                inner = both[:tile] + (both[tile:] + dot(left_split[held, :tile], feed_low[held]))
                high, low = split(inner)
                highs.append(high)
                lows.append(low)
            high = jnp.concatenate(highs, axis=1)
            both = dot(jnp.concatenate([high, jnp.concatenate(lows, axis=1)], axis=0), right_high[k])
            part[at(k)] = both[:tile] + (both[tile:] + dot(high, right_low[k]))
            return carry

        lax.fori_loop(0, blocks, block, 0)

    def to_partner(n, distance):
        owner = peer(distance) * 2 + 1 - column
        return pltpu.make_async_remote_copy(
            src_ref=part.at[rows(owner)], dst_ref=pair_in.at[n], send_sem=pair_send.at[n],
            recv_sem=pair_recv.at[n], device_id={"term": partner}, device_id_type=MESH,
        )

    def along_line(distance):
        return pltpu.make_async_remote_copy(
            src_ref=line_out.at[distance], dst_ref=line_in.at[distance], send_sem=line_send.at[distance],
            recv_sem=line_recv.at[distance], device_id={"term": peer(distance) * 2 + column},
            device_id_type=MESH,
        )

    def sum_out(distance):
        mine = rows(me)
        return pltpu.make_async_remote_copy(
            src_ref=search_image.at[mine], dst_ref=search_image.at[mine], send_sem=out_send.at[distance],
            recv_sem=out_recv.at[distance], device_id={"term": peer(distance) * 2 + column},
            device_id_type=MESH,
        )

    def sum_across(distance):
        held = rows(peer(places - distance) * 2 + column)
        return pltpu.make_async_remote_copy(
            src_ref=search_image.at[held], dst_ref=search_image.at[held], send_sem=across_send.at[distance],
            recv_sem=across_recv.at[distance], device_id={"term": partner}, device_id_type=MESH,
        )

    order = list(range(1, places)) + [0]

    def sum_terms():
        pairs = [to_partner(distance, distance) for distance in order]
        for copy in pairs:
            copy.start()
        lines = []
        for distance, copy in zip(order, pairs):
            copy.wait_recv()
            summed = pair_in[distance] + part[rows(peer(distance) * 2 + column)]
            if distance:
                line_out[distance] = summed
                lines.append(along_line(distance))
                lines[-1].start()
        for copy in lines:
            copy.wait_recv()
        for distance in range(1, places):
            summed = summed + line_in[distance]
        search_image[rows(me)] = summed
        outs = [sum_out(distance) for distance in range(1, places)]
        for copy in outs:
            copy.start()
        acrosses = [sum_across(distance) for distance in range(places)]
        acrosses[0].start()
        for distance in range(1, places):
            outs[distance - 1].wait_recv()
            acrosses[distance].start()
        for copy in acrosses:
            copy.wait_recv()
        for copy in pairs + lines + outs + acrosses:
            copy.wait_send()

    def step(iteration, energy):
        apply_local()
        sum_terms()
        first = iteration == 0
        def measures(k, sums):
            v, i, s, h = vector[at(k)], image[at(k)], search[at(k)], search_image[at(k)]
            return sums[0] + folded(v * h + s * i), sums[1] + folded(s * h)

        cross, own = lax.fori_loop(0, blocks, measures, (zero, zero))
        coupling, curvature = 0.5 * total_of(cross), total_of(own)
        half_gap = 0.5 * (energy - curvature)
        radius = jnp.sqrt(half_gap * half_gap + coupling * coupling)
        keep = jnp.where(
            half_gap >= 0, coupling * coupling / (radius + jnp.abs(half_gap)), radius - half_gap
        )
        norm = jnp.sqrt(keep * keep + coupling * coupling)
        keep, mix = jnp.where(first, 0.0, keep / norm), jnp.where(first, 1.0, -coupling / norm)
        def update(k, total):
            new_vector = keep * vector[at(k)] + mix * search[at(k)]
            new_image = keep * image[at(k)] + mix * search_image[at(k)]
            vector[at(k)] = new_vector
            image[at(k)] = new_image
            return total + folded(new_vector * new_image)

        energy = total_of(lax.fori_loop(0, blocks, update, zero))

        def scale_residual(k, total):
            scaled = (image[at(k)] - energy * vector[at(k)]) * inverse[at(k)]
            search[at(k)] = scaled
            return total + folded(vector[at(k)] * scaled)

        projection = total_of(lax.fori_loop(0, blocks, scale_residual, zero))

        def remove(k, total):
            remainder = search[at(k)] - projection * vector[at(k)]
            search[at(k)] = remainder
            return total + folded(remainder * remainder)

        store_search(1.0 / jnp.sqrt(total_of(lax.fori_loop(0, blocks, remove, zero)) + EPSILON))
        return energy

    energy = lax.fori_loop(0, ITERS + 1, step, jnp.zeros((1, 1), F32))
    energy_ref[...] = jnp.broadcast_to(energy, energy_ref.shape)
    scale = math.sqrt(blocks * tile * tile)
    for k in range(blocks):
        if share % 8 == 0:
            out_ref[k] = vector[pl.ds(pl.multiple_of(k * tile + me * share, 8), share)] * scale
        else:
            out_ref[k] = vector[k * tile:(k + 1) * tile] * scale


def shards(
    devices, segs,
    envs_left, envs_right, site_left, site_right, precondition, source_block, left_tile, right_tile,
):
    terms, tiles, tile = envs_left.shape[1], envs_left.shape[2], envs_left.shape[3]
    blocks = site_left.shape[1]
    piece = blocks * tile // devices
    places = devices // 2
    share = tile // devices
    out_rows = share if share % 8 == 0 else tile
    flat = pltpu.VMEM((blocks * tile, tile), F32)
    stack = pltpu.VMEM((blocks, tile, tile), F32)
    slots = pltpu.VMEM((places, piece, tile), F32)
    sems = pltpu.SemaphoreType.DMA((places,))
    hbm = pl.BlockSpec(memory_space=pl.ANY)
    smem = pl.BlockSpec(memory_space=pltpu.SMEM)
    vmem = pl.BlockSpec(memory_space=pltpu.VMEM)
    out, energy = pl.pallas_call(
        functools.partial(kernel, devices, segs, blocks, tile, terms, share),
        out_shape=(
            jax.ShapeDtypeStruct((blocks, out_rows, tile), F32),
            jax.ShapeDtypeStruct((8, 128), F32),
        ),
        in_specs=[hbm] * 5 + [smem] * 3,
        out_specs=(vmem, vmem),
        scratch_shapes=[
            pltpu.VMEM((terms, tiles, tile, tile), F32),
            pltpu.VMEM((terms, tiles, tile, tile), F32),
            stack,
            stack,
            pltpu.VMEM((blocks, tile * tile), F32),
            pltpu.VMEM((terms * blocks, 2 * tile, tile), BF16),
            pltpu.VMEM((blocks, terms * tile, tile), BF16),
            pltpu.VMEM((blocks, terms * tile, tile), BF16),
            pltpu.VMEM((blocks, tile, tile), BF16),
            pltpu.VMEM((blocks, tile, tile), BF16),
            pltpu.VMEM((terms * blocks, tile, tile), F32),
            pltpu.VMEM((terms * blocks, tile, tile), BF16),
            pltpu.VMEM((terms * blocks, tile, tile), BF16),
            flat, flat, flat, flat, flat, flat,
            slots, slots, slots,
            pltpu.SemaphoreType.DMA((3,)),
            pltpu.SemaphoreType.DMA((2,)),
            pltpu.SemaphoreType.DMA((2,)),
            sems, sems, sems, sems, sems, sems, sems, sems,
        ],
        compiler_params=pltpu.CompilerParams(
            collective_id=0, has_side_effects=True, vmem_limit_bytes=40 * 1024 * 1024
        ),
    )(
        envs_left[0], envs_right[0], site_left[0], site_right[0], precondition[0],
        source_block[0], left_tile[0], right_tile[0],
    )
    if out_rows != share:
        out = lax.dynamic_slice_in_dim(out, lax.axis_index("term") * share, share, 1)
    return (out.reshape(1, blocks, share * tile), energy[0, :1])


def solution(mesh):
    in_specs = (
        P("seg", "term", None, None, None),
        P("seg", "term", None, None, None),
        P("seg", None, None, None),
        P("seg", None, None, None),
        P("seg", None, None),
        P("seg", "term", None),
        P("seg", None),
        P("seg", None),
    )
    out_specs = (P("seg", None, "term"), P("seg"))
    body = functools.partial(shards, mesh.shape["term"], mesh.shape["seg"])
    return jax.shard_map(body, mesh=mesh, in_specs=in_specs, out_specs=out_specs, check_vma=False)
```

```python
import functools
import math

import jax
import jax.numpy as jnp
from jax import lax
from jax.experimental import pallas as pl
from jax.experimental.pallas import tpu as pltpu
from jax.sharding import PartitionSpec as P

ITERS = 4
PARTS = (3, 2, 1)
EPSILON = 1e-06
MESH = pl.DeviceIdType.MESH
F32 = jnp.float32
BF16 = jnp.bfloat16


def split(value):
    high = value.astype(BF16)
    low = (value - high.astype(F32)).astype(BF16)
    return high, low


def dot(a, b):
    return lax.dot_general(a, b, (((1,), (0,)), ((), ())), preferred_element_type=F32)


def total_of(value):
    return jnp.sum(jnp.sum(value, axis=0, keepdims=True), axis=1, keepdims=True)


def folded(value):
    return jnp.sum(value.reshape(value.shape[0] // 8, 8, value.shape[1]), axis=0)


def kernel(
    devices, segs, blocks, tile, terms, share, parts,
    left_hbm, right_hbm, site_left_hbm, site_right_hbm, precond_hbm, sources, left_ids, right_ids,
    out_ref, energy_ref,
    left, right, site_left, site_right, precond, left_split, right_high, right_low,
    search_high, search_low, picked, feed_high, feed_low, inverse, search, vector, image, search_image, part, pair_in, line_out, line_in,
    local_sems, seg_send, seg_recv, pair_send, pair_recv, line_send, line_recv,
    out_send, out_recv, across_send, across_recv,
):
    me = lax.axis_index("term")
    seg = lax.axis_index("seg")
    column, place = me % 2, me // 2
    places = devices // 2
    partner = place * 2 + 1 - column
    before, after = (seg + segs - 1) % segs, (seg + 1) % segs
    piece = blocks * tile // (parts * devices)

    def rows(part_id, owner):
        return pl.ds(pl.multiple_of((part_id * devices + owner) * piece, 8), piece)

    def peer(distance):
        return (place + distance) % places

    locals_ = [
        pltpu.make_async_copy(source, target, local_sems.at[n])
        for n, (source, target) in enumerate(
            [(site_left_hbm, site_left), (left_hbm, left), (precond_hbm, precond)]
        )
    ]
    for copy in locals_:
        copy.start()

    barrier = pltpu.get_barrier_semaphore()
    pl.semaphore_signal(barrier, inc=1, device_id={"seg": before}, device_id_type=MESH)
    pl.semaphore_signal(barrier, inc=1, device_id={"seg": after}, device_id_type=MESH)
    pl.semaphore_signal(barrier, inc=1, device_id={"term": partner}, device_id_type=MESH)
    for distance in range(1, places):
        pl.semaphore_signal(
            barrier, inc=1, device_id={"term": peer(distance) * 2 + column}, device_id_type=MESH
        )
    pl.semaphore_wait(barrier, places + 2)

    seg_copies = [
        pltpu.make_async_remote_copy(
            src_ref=source, dst_ref=target, send_sem=seg_send.at[n], recv_sem=seg_recv.at[n],
            device_id={"seg": before}, device_id_type=MESH,
        )
        for n, (source, target) in enumerate(
            [(site_right_hbm.at[rows(h, me)], site_right.at[rows(h, me)]) for h in range(parts)]
            + [(right_hbm, right)]
        )
    ]
    for copy in seg_copies:
        copy.start()

    def send_out(buffer, h, distance):
        mine = rows(h, me)
        return pltpu.make_async_remote_copy(
            src_ref=buffer.at[mine], dst_ref=buffer.at[mine], send_sem=out_send.at[h * places + distance],
            recv_sem=out_recv.at[h * places + distance],
            device_id={"term": peer(distance) * 2 + column}, device_id_type=MESH,
        )

    def send_across(buffer, h, distance):
        held = rows(h, peer(places - distance) * 2 + column)
        return pltpu.make_async_remote_copy(
            src_ref=buffer.at[held], dst_ref=buffer.at[held], send_sem=across_send.at[h * places + distance],
            recv_sem=across_recv.at[h * places + distance], device_id={"term": partner}, device_id_type=MESH,
        )

    def spread(buffer, ready):
        outs, acrosses = [], []
        for h in range(parts):
            ready(h)
            outs.append([send_out(buffer, h, distance) for distance in range(1, places)])
            acrosses.append([send_across(buffer, h, distance) for distance in range(places)])
            for copy in outs[h] + acrosses[h][:1]:
                copy.start()
        for h in range(parts):
            for distance in range(1, places):
                outs[h][distance - 1].wait_recv()
                acrosses[h][distance].start()
        for h in range(parts):
            for copy in acrosses[h]:
                copy.wait_recv()
        for h in range(parts):
            for copy in outs[h] + acrosses[h]:
                copy.wait_send()

    locals_[1].wait()
    def pick_left(k, carry):
        for t in range(terms):
            picked[t * blocks + k] = left[t, left_ids[k]] * (sources[t, k] >= 0).astype(F32)
        return carry

    lax.fori_loop(0, blocks, pick_left, 0)

    def split_left(n, carry):
        high, low = split(picked[n])
        left_split[n, :tile] = high
        left_split[n, tile:] = low
        return carry

    lax.fori_loop(0, terms * blocks, split_left, 0)
    locals_[2].wait()
    for k in range(blocks):
        inverse[k * tile:(k + 1) * tile] = 1.0 / precond[k:k + 1, :].reshape(tile, tile)
    vector[...] = jnp.zeros_like(vector)
    image[...] = jnp.zeros_like(image)

    zero = jnp.zeros((8, tile), F32)

    def at(k):
        return pl.ds(pl.multiple_of(k * tile, tile), tile)

    def store_search(length):
        def block(k, carry):
            value = search[at(k)] * length
            search[at(k)] = value
            high, low = split(value)
            search_high[k] = high
            search_low[k] = low
            return carry

        lax.fori_loop(0, blocks, block, 0)

    locals_[0].wait()
    spread(site_right, lambda h: seg_copies[h].wait())
    def guess(k, total):
        a_high, a_low = split(site_left[k])
        b_high, b_low = split(site_right[at(k)])
        value = dot(a_high, b_high) + (dot(a_high, b_low) + dot(a_low, b_high))
        search[at(k)] = value
        return total + folded(value * value)

    store_search(1.0 / jnp.sqrt(total_of(lax.fori_loop(0, blocks, guess, zero)) + EPSILON))

    seg_copies[parts].wait()
    def pick_right(k, carry):
        for t in range(terms):
            picked[t * blocks + k] = right[t, right_ids[k]]
        return carry

    lax.fori_loop(0, blocks, pick_right, 0)

    def split_right(k, carry):
        for t in range(terms):
            high, low = split(picked[t * blocks + k].T)
            right_high[k, t * tile:(t + 1) * tile] = high
            right_low[k, t * tile:(t + 1) * tile] = low
        return carry

    lax.fori_loop(0, blocks, split_right, 0)

    def apply_local(low_block, high_block):
        def pick(k, carry):
            for t in range(terms):
                source = jnp.maximum(sources[t, k], 0)
                feed_high[t * blocks + k] = search_high[source]
                feed_low[t * blocks + k] = search_low[source]
            return carry

        lax.fori_loop(low_block, high_block, pick, 0)

        def block(k, carry):
            highs, lows = [], []
            for t in range(terms):
                held = t * blocks + k
                both = dot(left_split[held], feed_high[held])
                inner = both[:tile] + (both[tile:] + dot(left_split[held, :tile], feed_low[held]))
                high, low = split(inner)
                highs.append(high)
                lows.append(low)
            high = jnp.concatenate(highs, axis=1)
            both = dot(jnp.concatenate([high, jnp.concatenate(lows, axis=1)], axis=0), right_high[k])
            part[at(k)] = both[:tile] + (both[tile:] + dot(high, right_low[k]))
            return carry

        lax.fori_loop(low_block, high_block, block, 0)

    def to_partner(h, distance):
        slot = h * places + distance
        return pltpu.make_async_remote_copy(
            src_ref=part.at[rows(h, peer(distance) * 2 + 1 - column)], dst_ref=pair_in.at[slot],
            send_sem=pair_send.at[slot], recv_sem=pair_recv.at[slot],
            device_id={"term": partner}, device_id_type=MESH,
        )

    def along_line(h, distance):
        slot = h * places + distance
        return pltpu.make_async_remote_copy(
            src_ref=line_out.at[slot], dst_ref=line_in.at[slot], send_sem=line_send.at[slot],
            recv_sem=line_recv.at[slot], device_id={"term": peer(distance) * 2 + column},
            device_id_type=MESH,
        )

    order = list(range(1, places)) + [0]

    def apply():
        pairs, lines = [], []
        for h in range(parts):
            apply_local(h * blocks // parts, (h + 1) * blocks // parts)
            pairs.append([to_partner(h, distance) for distance in order])
            for copy in pairs[h]:
                copy.start()
        for h in range(parts):
            lines.append([])
            for distance, copy in zip(order, pairs[h]):
                copy.wait_recv()
                slot = h * places + distance
                line_out[slot] = pair_in[slot] + part[rows(h, peer(distance) * 2 + column)]
                if distance:
                    lines[h].append(along_line(h, distance))
                    lines[h][-1].start()

        def finish(h):
            for copy in lines[h]:
                copy.wait_recv()
            summed = line_out[h * places]
            for distance in range(1, places):
                summed = summed + line_in[h * places + distance]
            search_image[rows(h, me)] = summed

        spread(search_image, finish)
        for h in range(parts):
            for copy in pairs[h] + lines[h]:
                copy.wait_send()

    def step(iteration, energy):
        apply()
        first = iteration == 0
        def measures(k, sums):
            v, i, s, h = vector[at(k)], image[at(k)], search[at(k)], search_image[at(k)]
            return sums[0] + folded(v * h + s * i), sums[1] + folded(s * h)

        cross, own = lax.fori_loop(0, blocks, measures, (zero, zero))
        coupling, curvature = 0.5 * total_of(cross), total_of(own)
        half_gap = 0.5 * (energy - curvature)
        radius = jnp.sqrt(half_gap * half_gap + coupling * coupling)
        keep = jnp.where(
            half_gap >= 0, coupling * coupling / (radius + jnp.abs(half_gap)), radius - half_gap
        )
        norm = jnp.sqrt(keep * keep + coupling * coupling)
        keep, mix = jnp.where(first, 0.0, keep / norm), jnp.where(first, 1.0, -coupling / norm)
        def update(k, total):
            new_vector = keep * vector[at(k)] + mix * search[at(k)]
            new_image = keep * image[at(k)] + mix * search_image[at(k)]
            vector[at(k)] = new_vector
            image[at(k)] = new_image
            return total + folded(new_vector * new_image)

        energy = total_of(lax.fori_loop(0, blocks, update, zero))

        def scale_residual(k, total):
            scaled = (image[at(k)] - energy * vector[at(k)]) * inverse[at(k)]
            search[at(k)] = scaled
            return total + folded(vector[at(k)] * scaled)

        projection = total_of(lax.fori_loop(0, blocks, scale_residual, zero))

        def remove(k, total):
            remainder = search[at(k)] - projection * vector[at(k)]
            search[at(k)] = remainder
            return total + folded(remainder * remainder)

        store_search(1.0 / jnp.sqrt(total_of(lax.fori_loop(0, blocks, remove, zero)) + EPSILON))
        return energy

    energy = lax.fori_loop(0, ITERS + 1, step, jnp.zeros((1, 1), F32))
    energy_ref[...] = jnp.broadcast_to(energy, energy_ref.shape)
    scale = math.sqrt(blocks * tile * tile)
    for k in range(blocks):
        if share % 8 == 0:
            out_ref[k] = vector[pl.ds(pl.multiple_of(k * tile + me * share, 8), share)] * scale
        else:
            out_ref[k] = vector[k * tile:(k + 1) * tile] * scale


def shards(
    devices, segs,
    envs_left, envs_right, site_left, site_right, precondition, source_block, left_tile, right_tile,
):
    terms, tiles, tile = envs_left.shape[1], envs_left.shape[2], envs_left.shape[3]
    blocks = site_left.shape[1]
    piece = blocks * tile // devices
    parts = next(n for n in PARTS if blocks % n == 0 and piece % (8 * n) == 0)
    places = devices // 2
    share = tile // devices
    out_rows = share if share % 8 == 0 else tile
    flat = pltpu.VMEM((blocks * tile, tile), F32)
    stack = pltpu.VMEM((blocks, tile, tile), F32)
    slots = pltpu.VMEM((parts * places, piece // parts, tile), F32)
    sems = pltpu.SemaphoreType.DMA((parts * places,))
    hbm = pl.BlockSpec(memory_space=pl.ANY)
    smem = pl.BlockSpec(memory_space=pltpu.SMEM)
    vmem = pl.BlockSpec(memory_space=pltpu.VMEM)
    out, energy = pl.pallas_call(
        functools.partial(kernel, devices, segs, blocks, tile, terms, share, parts),
        out_shape=(
            jax.ShapeDtypeStruct((blocks, out_rows, tile), F32),
            jax.ShapeDtypeStruct((8, 128), F32),
        ),
        in_specs=[hbm] * 5 + [smem] * 3,
        out_specs=(vmem, vmem),
        scratch_shapes=[
            pltpu.VMEM((terms, tiles, tile, tile), F32),
            pltpu.VMEM((terms, tiles, tile, tile), F32),
            stack,
            flat,
            pltpu.VMEM((blocks, tile * tile), F32),
            pltpu.VMEM((terms * blocks, 2 * tile, tile), BF16),
            pltpu.VMEM((blocks, terms * tile, tile), BF16),
            pltpu.VMEM((blocks, terms * tile, tile), BF16),
            pltpu.VMEM((blocks, tile, tile), BF16),
            pltpu.VMEM((blocks, tile, tile), BF16),
            pltpu.VMEM((terms * blocks, tile, tile), F32),
            pltpu.VMEM((terms * blocks, tile, tile), BF16),
            pltpu.VMEM((terms * blocks, tile, tile), BF16),
            flat, flat, flat, flat, flat, flat,
            slots, slots, slots,
            pltpu.SemaphoreType.DMA((3,)),
            pltpu.SemaphoreType.DMA((parts + 1,)),
            pltpu.SemaphoreType.DMA((parts + 1,)),
            sems, sems, sems, sems, sems, sems, sems, sems,
        ],
        compiler_params=pltpu.CompilerParams(
            collective_id=0, has_side_effects=True, vmem_limit_bytes=40 * 1024 * 1024
        ),
    )(
        envs_left[0], envs_right[0], site_left[0], site_right[0].reshape(blocks * tile, tile), precondition[0],
        source_block[0], left_tile[0], right_tile[0],
    )
    if out_rows != share:
        out = lax.dynamic_slice_in_dim(out, lax.axis_index("term") * share, share, 1)
    return (out.reshape(1, blocks, share * tile), energy[0, :1])


def solution(mesh):
    in_specs = (
        P("seg", "term", None, None, None),
        P("seg", "term", None, None, None),
        P("seg", None, None, None),
        P("seg", None, None, None),
        P("seg", None, None),
        P("seg", "term", None),
        P("seg", None),
        P("seg", None),
    )
    out_specs = (P("seg", None, "term"), P("seg"))
    body = functools.partial(shards, mesh.shape["term"], mesh.shape["seg"])
    return jax.shard_map(body, mesh=mesh, in_specs=in_specs, out_specs=out_specs, check_vma=False)
```

```python
import functools
import math

import jax
import jax.numpy as jnp
from jax import lax
from jax.experimental import pallas as pl
from jax.experimental.pallas import tpu as pltpu
from jax.sharding import PartitionSpec as P

ITERS = 4
PARTS = (6, 3, 2, 1)
EPSILON = 1e-06
MESH = pl.DeviceIdType.MESH
F32 = jnp.float32
BF16 = jnp.bfloat16


def split(value):
    high = value.astype(BF16)
    low = (value - high.astype(F32)).astype(BF16)
    return high, low


def dot(a, b):
    return lax.dot_general(a, b, (((1,), (0,)), ((), ())), preferred_element_type=F32)


def total_of(value):
    return jnp.sum(jnp.sum(value, axis=0, keepdims=True), axis=1, keepdims=True)


def folded(value):
    return jnp.sum(value.reshape(value.shape[0] // 8, 8, value.shape[1]), axis=0)


def kernel(
    devices, segs, blocks, tile, terms, share, parts,
    left_hbm, right_hbm, site_left_hbm, site_right_hbm, precond_hbm, sources, left_ids, right_ids,
    out_ref, energy_ref,
    left, right, site_left, site_right, precond, left_split, right_high, right_low,
    search_high, search_low, picked, feed_high, feed_low, inverse, search, vector, image, search_image, part, pair_in, line_out, line_in,
    local_sems, seg_send, seg_recv, pair_send, pair_recv, line_send, line_recv,
    out_send, out_recv, across_send, across_recv,
):
    me = lax.axis_index("term")
    seg = lax.axis_index("seg")
    column, place = me % 2, me // 2
    places = devices // 2
    partner = place * 2 + 1 - column
    before, after = (seg + segs - 1) % segs, (seg + 1) % segs
    piece = blocks * tile // (parts * devices)

    def rows(part_id, owner):
        return pl.ds(pl.multiple_of((part_id * devices + owner) * piece, 8), piece)

    def at(k):
        return pl.ds(pl.multiple_of(k * tile, tile), tile)

    def peer(distance):
        return (place + distance) % places

    locals_ = [
        pltpu.make_async_copy(source, target, local_sems.at[n])
        for n, (source, target) in enumerate(
            [(site_left_hbm, site_left), (left_hbm, left), (precond_hbm, precond)]
        )
    ]
    for copy in locals_:
        copy.start()

    barrier = pltpu.get_barrier_semaphore()
    pl.semaphore_signal(barrier, inc=1, device_id={"seg": before}, device_id_type=MESH)
    pl.semaphore_signal(barrier, inc=1, device_id={"seg": after}, device_id_type=MESH)
    pl.semaphore_signal(barrier, inc=1, device_id={"term": partner}, device_id_type=MESH)
    for distance in range(1, places):
        pl.semaphore_signal(
            barrier, inc=1, device_id={"term": peer(distance) * 2 + column}, device_id_type=MESH
        )
    pl.semaphore_wait(barrier, places + 2)

    seg_copies = [
        pltpu.make_async_remote_copy(
            src_ref=source, dst_ref=target, send_sem=seg_send.at[n], recv_sem=seg_recv.at[n],
            device_id={"seg": before}, device_id_type=MESH,
        )
        for n, (source, target) in enumerate(
            [(site_right_hbm.at[rows(h, me)], site_right.at[rows(h, me)]) for h in range(parts)]
            + [(right_hbm.at[t], right.at[t]) for t in range(terms)]
        )
    ]
    for copy in seg_copies:
        copy.start()

    def send_out(buffer, h, distance):
        mine = rows(h, me)
        return pltpu.make_async_remote_copy(
            src_ref=buffer.at[mine], dst_ref=buffer.at[mine], send_sem=out_send.at[h * places + distance],
            recv_sem=out_recv.at[h * places + distance],
            device_id={"term": peer(distance) * 2 + column}, device_id_type=MESH,
        )

    def send_across(buffer, h, distance):
        held = rows(h, peer(places - distance) * 2 + column)
        return pltpu.make_async_remote_copy(
            src_ref=buffer.at[held], dst_ref=buffer.at[held], send_sem=across_send.at[h * places + distance],
            recv_sem=across_recv.at[h * places + distance], device_id={"term": partner}, device_id_type=MESH,
        )

    def spread(buffer, ready):
        outs, acrosses = [], []
        for h in range(parts):
            ready(h)
            outs.append([send_out(buffer, h, distance) for distance in range(1, places)])
            acrosses.append([send_across(buffer, h, distance) for distance in range(places)])
            for copy in outs[h] + acrosses[h][:1]:
                copy.start()
        for h in range(parts):
            for distance in range(1, places):
                outs[h][distance - 1].wait_recv()
                acrosses[h][distance].start()
        for h in range(parts):
            for copy in acrosses[h]:
                copy.wait_recv()
        for h in range(parts):
            for copy in outs[h] + acrosses[h]:
                copy.wait_send()

    locals_[1].wait()
    def pick_left(k, carry):
        for t in range(terms):
            picked[t * blocks + k] = left[t, left_ids[k]] * (sources[t, k] >= 0).astype(F32)
        return carry

    lax.fori_loop(0, blocks, pick_left, 0)

    def split_left(n, carry):
        high, low = split(picked[n])
        left_split[n, :tile] = high
        left_split[n, tile:] = low
        return carry

    lax.fori_loop(0, terms * blocks, split_left, 0)
    locals_[2].wait()
    for k in range(blocks):
        inverse[at(k)] = 1.0 / precond[at(k)]
    vector[...] = jnp.zeros_like(vector)
    image[...] = jnp.zeros_like(image)

    zero = jnp.zeros((8, tile), F32)

    def store_search(length):
        def block(k, carry):
            value = search[at(k)] * length
            search[at(k)] = value
            high, low = split(value)
            search_high[k] = high
            search_low[k] = low
            return carry

        lax.fori_loop(0, blocks, block, 0)

    locals_[0].wait()
    spread(site_right, lambda h: seg_copies[h].wait())
    def guess(k, total):
        a_high, a_low = split(site_left[k])
        b_high, b_low = split(site_right[at(k)])
        value = dot(a_high, b_high) + (dot(a_high, b_low) + dot(a_low, b_high))
        search[at(k)] = value
        return total + folded(value * value)

    store_search(1.0 / jnp.sqrt(total_of(lax.fori_loop(0, blocks, guess, zero)) + EPSILON))

    for t in range(terms):
        seg_copies[parts + t].wait()
    for t in range(terms):

        def pick_right(k, carry):
            picked[k] = right[t, right_ids[k]]
            return carry

        lax.fori_loop(0, blocks, pick_right, 0)

        def split_right(k, carry):
            high, low = split(picked[k].T)
            right_high[k, t * tile:(t + 1) * tile] = high
            right_low[k, t * tile:(t + 1) * tile] = low
            return carry

        lax.fori_loop(0, blocks, split_right, 0)

    def apply_local(low_block, high_block):
        def pick(k, carry):
            for t in range(terms):
                source = jnp.maximum(sources[t, k], 0)
                feed_high[t * blocks + k] = search_high[source]
                feed_low[t * blocks + k] = search_low[source]
            return carry

        lax.fori_loop(low_block, high_block, pick, 0)

        def block(k, carry):
            highs, lows = [], []
            for t in range(terms):
                held = t * blocks + k
                both = dot(left_split[held], feed_high[held])
                inner = both[:tile] + (both[tile:] + dot(left_split[held, :tile], feed_low[held]))
                high, low = split(inner)
                highs.append(high)
                lows.append(low)
            high = jnp.concatenate(highs, axis=1)
            both = dot(jnp.concatenate([high, jnp.concatenate(lows, axis=1)], axis=0), right_high[k])
            part[at(k)] = both[:tile] + (both[tile:] + dot(high, right_low[k]))
            return carry

        lax.fori_loop(low_block, high_block, block, 0)

    def to_partner(h, distance):
        slot = h * places + distance
        return pltpu.make_async_remote_copy(
            src_ref=part.at[rows(h, peer(distance) * 2 + 1 - column)], dst_ref=pair_in.at[slot],
            send_sem=pair_send.at[slot], recv_sem=pair_recv.at[slot],
            device_id={"term": partner}, device_id_type=MESH,
        )

    def along_line(h, distance):
        slot = h * places + distance
        return pltpu.make_async_remote_copy(
            src_ref=line_out.at[slot], dst_ref=line_in.at[slot], send_sem=line_send.at[slot],
            recv_sem=line_recv.at[slot], device_id={"term": peer(distance) * 2 + column},
            device_id_type=MESH,
        )

    order = list(range(1, places)) + [0]

    def apply():
        pairs, lines = [], []
        for h in range(parts):
            apply_local(h * blocks // parts, (h + 1) * blocks // parts)
            pairs.append([to_partner(h, distance) for distance in order])
            for copy in pairs[h]:
                copy.start()
        for h in range(parts):
            lines.append([])
            for distance, copy in zip(order, pairs[h]):
                copy.wait_recv()
                slot = h * places + distance
                line_out[slot] = pair_in[slot] + part[rows(h, peer(distance) * 2 + column)]
                if distance:
                    lines[h].append(along_line(h, distance))
                    lines[h][-1].start()

        def finish(h):
            for copy in lines[h]:
                copy.wait_recv()
            summed = line_out[h * places]
            for distance in range(1, places):
                summed = summed + line_in[h * places + distance]
            search_image[rows(h, me)] = summed

        spread(search_image, finish)
        for h in range(parts):
            for copy in pairs[h] + lines[h]:
                copy.wait_send()

    def step(iteration, energy):
        apply()
        first = iteration == 0
        def measures(k, sums):
            v, i, s, h = vector[at(k)], image[at(k)], search[at(k)], search_image[at(k)]
            return sums[0] + folded(v * h + s * i), sums[1] + folded(s * h)

        cross, own = lax.fori_loop(0, blocks, measures, (zero, zero))
        coupling, curvature = 0.5 * total_of(cross), total_of(own)
        half_gap = 0.5 * (energy - curvature)
        radius = jnp.sqrt(half_gap * half_gap + coupling * coupling)
        keep = jnp.where(
            half_gap >= 0, coupling * coupling / (radius + jnp.abs(half_gap)), radius - half_gap
        )
        norm = jnp.sqrt(keep * keep + coupling * coupling)
        keep, mix = jnp.where(first, 0.0, keep / norm), jnp.where(first, 1.0, -coupling / norm)
        def update(k, total):
            new_vector = keep * vector[at(k)] + mix * search[at(k)]
            new_image = keep * image[at(k)] + mix * search_image[at(k)]
            vector[at(k)] = new_vector
            image[at(k)] = new_image
            return total + folded(new_vector * new_image)

        energy = total_of(lax.fori_loop(0, blocks, update, zero))

        def scale_residual(k, total):
            scaled = (image[at(k)] - energy * vector[at(k)]) * inverse[at(k)]
            search[at(k)] = scaled
            return total + folded(vector[at(k)] * scaled)

        projection = total_of(lax.fori_loop(0, blocks, scale_residual, zero))

        def remove(k, total):
            remainder = search[at(k)] - projection * vector[at(k)]
            search[at(k)] = remainder
            return total + folded(remainder * remainder)

        store_search(1.0 / jnp.sqrt(total_of(lax.fori_loop(0, blocks, remove, zero)) + EPSILON))
        return energy

    energy = lax.fori_loop(0, ITERS + 1, step, jnp.zeros((1, 1), F32))
    energy_ref[...] = jnp.broadcast_to(energy, energy_ref.shape)
    scale = math.sqrt(blocks * tile * tile)
    for k in range(blocks):
        if share % 8 == 0:
            out_ref[k] = vector[pl.ds(pl.multiple_of(k * tile + me * share, 8), share)] * scale
        else:
            out_ref[k] = vector[k * tile:(k + 1) * tile] * scale


def shards(
    devices, segs,
    envs_left, envs_right, site_left, site_right, precondition, source_block, left_tile, right_tile,
):
    terms, tiles, tile = envs_left.shape[1], envs_left.shape[2], envs_left.shape[3]
    blocks = site_left.shape[1]
    piece = blocks * tile // devices
    parts = next(n for n in PARTS if blocks % n == 0 and piece % (8 * n) == 0)
    places = devices // 2
    share = tile // devices
    out_rows = share if share % 8 == 0 else tile
    flat = pltpu.VMEM((blocks * tile, tile), F32)
    stack = pltpu.VMEM((blocks, tile, tile), F32)
    slots = pltpu.VMEM((parts * places, piece // parts, tile), F32)
    sems = pltpu.SemaphoreType.DMA((parts * places,))
    hbm = pl.BlockSpec(memory_space=pl.ANY)
    smem = pl.BlockSpec(memory_space=pltpu.SMEM)
    vmem = pl.BlockSpec(memory_space=pltpu.VMEM)
    out, energy = pl.pallas_call(
        functools.partial(kernel, devices, segs, blocks, tile, terms, share, parts),
        out_shape=(
            jax.ShapeDtypeStruct((blocks, out_rows, tile), F32),
            jax.ShapeDtypeStruct((8, 128), F32),
        ),
        in_specs=[hbm] * 5 + [smem] * 3,
        out_specs=(vmem, vmem),
        scratch_shapes=[
            pltpu.VMEM((terms, tiles, tile, tile), F32),
            pltpu.VMEM((terms, tiles, tile, tile), F32),
            stack,
            flat,
            flat,
            pltpu.VMEM((terms * blocks, 2 * tile, tile), BF16),
            pltpu.VMEM((blocks, terms * tile, tile), BF16),
            pltpu.VMEM((blocks, terms * tile, tile), BF16),
            pltpu.VMEM((blocks, tile, tile), BF16),
            pltpu.VMEM((blocks, tile, tile), BF16),
            pltpu.VMEM((terms * blocks, tile, tile), F32),
            pltpu.VMEM((terms * blocks, tile, tile), BF16),
            pltpu.VMEM((terms * blocks, tile, tile), BF16),
            flat, flat, flat, flat, flat, flat,
            slots, slots, slots,
            pltpu.SemaphoreType.DMA((3,)),
            pltpu.SemaphoreType.DMA((parts + terms,)),
            pltpu.SemaphoreType.DMA((parts + terms,)),
            sems, sems, sems, sems, sems, sems, sems, sems,
        ],
        compiler_params=pltpu.CompilerParams(
            collective_id=0, has_side_effects=True
        ),
    )(
        envs_left[0], envs_right[0], site_left[0], site_right[0].reshape(blocks * tile, tile), precondition.reshape(blocks * tile, tile),
        source_block[0], left_tile[0], right_tile[0],
    )
    if out_rows != share:
        out = lax.dynamic_slice_in_dim(out, lax.axis_index("term") * share, share, 1)
    return (out.reshape(1, blocks, share * tile), energy[0, :1])


def solution(mesh):
    in_specs = (
        P("seg", "term", None, None, None),
        P("seg", "term", None, None, None),
        P("seg", None, None, None),
        P("seg", None, None, None),
        P("seg", None, None),
        P("seg", "term", None),
        P("seg", None),
        P("seg", None),
    )
    out_specs = (P("seg", None, "term"), P("seg"))
    body = functools.partial(shards, mesh.shape["term"], mesh.shape["seg"])
    return jax.shard_map(body, mesh=mesh, in_specs=in_specs, out_specs=out_specs, check_vma=False)
```

```python
import functools
import math

import jax
import jax.numpy as jnp
from jax import lax
from jax.experimental import pallas as pl
from jax.experimental.pallas import tpu as pltpu
from jax.sharding import PartitionSpec as P

ITERS = 4
PARTS = (6, 3, 2, 1)
EPSILON = 1e-06
MESH = pl.DeviceIdType.MESH
F32 = jnp.float32
BF16 = jnp.bfloat16


def split(value):
    high = value.astype(BF16)
    low = (value - high.astype(F32)).astype(BF16)
    return high, low


def dot(a, b):
    return lax.dot_general(a, b, (((1,), (0,)), ((), ())), preferred_element_type=F32)


def total_of(value):
    return jnp.sum(jnp.sum(value, axis=0, keepdims=True), axis=1, keepdims=True)


def folded(value):
    return jnp.sum(value.reshape(value.shape[0] // 8, 8, value.shape[1]), axis=0)


def kernel(
    devices, segs, blocks, tile, terms, share, parts,
    left_hbm, right_hbm, site_left_hbm, site_right_hbm, precond_hbm, sources, left_ids, right_ids,
    out_ref, energy_ref,
    left, right, site_left, site_right, precond, left_split, right_high, right_low,
    search_high, search_low, picked, feed_high, feed_low, inverse, search, vector, image, search_image, part, pair_in, line_out, line_in,
    local_sems, seg_send, seg_recv, pair_send, pair_recv, line_send, line_recv,
    out_send, out_recv, across_send, across_recv,
):
    me = lax.axis_index("term")
    seg = lax.axis_index("seg")
    column, place = me % 2, me // 2
    places = devices // 2
    partner = place * 2 + 1 - column
    before, after = (seg + segs - 1) % segs, (seg + 1) % segs
    piece = blocks * tile // (parts * devices)

    def rows(part_id, owner):
        return pl.ds(pl.multiple_of((part_id * devices + owner) * piece, 8), piece)

    def at(k):
        return pl.ds(pl.multiple_of(k * tile, tile), tile)

    def peer(distance):
        return (place + distance) % places

    locals_ = [
        pltpu.make_async_copy(source, target, local_sems.at[n])
        for n, (source, target) in enumerate(
            [(site_left_hbm, site_left), (left_hbm, left), (precond_hbm, precond)]
        )
    ]
    for copy in locals_:
        copy.start()

    barrier = pltpu.get_barrier_semaphore()
    pl.semaphore_signal(barrier, inc=1, device_id={"seg": before}, device_id_type=MESH)
    pl.semaphore_signal(barrier, inc=1, device_id={"seg": after}, device_id_type=MESH)
    pl.semaphore_signal(barrier, inc=1, device_id={"term": partner}, device_id_type=MESH)
    for distance in range(1, places):
        pl.semaphore_signal(
            barrier, inc=1, device_id={"term": peer(distance) * 2 + column}, device_id_type=MESH
        )
    pl.semaphore_wait(barrier, places + 2)

    seg_copies = [
        pltpu.make_async_remote_copy(
            src_ref=source, dst_ref=target, send_sem=seg_send.at[n], recv_sem=seg_recv.at[n],
            device_id={"seg": before}, device_id_type=MESH,
        )
        for n, (source, target) in enumerate(
            [(site_right_hbm.at[rows(h, me)], site_right.at[rows(h, me)]) for h in range(parts)]
            + [(right_hbm.at[t], right.at[t]) for t in range(terms)]
        )
    ]
    for copy in seg_copies:
        copy.start()

    def send_out(buffer, h, distance):
        mine = rows(h, me)
        return pltpu.make_async_remote_copy(
            src_ref=buffer.at[mine], dst_ref=buffer.at[mine], send_sem=out_send.at[h * places + distance],
            recv_sem=out_recv.at[h * places + distance],
            device_id={"term": peer(distance) * 2 + column}, device_id_type=MESH,
        )

    def send_across(buffer, h, distance):
        held = rows(h, peer(places - distance) * 2 + column)
        return pltpu.make_async_remote_copy(
            src_ref=buffer.at[held], dst_ref=buffer.at[held], send_sem=across_send.at[h * places + distance],
            recv_sem=across_recv.at[h * places + distance], device_id={"term": partner}, device_id_type=MESH,
        )

    def spread(buffer, ready):
        outs, acrosses = [], []
        for h in range(parts):
            ready(h)
            outs.append([send_out(buffer, h, distance) for distance in range(1, places)])
            acrosses.append([send_across(buffer, h, distance) for distance in range(places)])
            for copy in outs[h] + acrosses[h][:1]:
                copy.start()
        for h in range(parts):
            for distance in range(1, places):
                outs[h][distance - 1].wait_recv()
                acrosses[h][distance].start()
        for h in range(parts):
            for copy in acrosses[h]:
                copy.wait_recv()
        for h in range(parts):
            for copy in outs[h] + acrosses[h]:
                copy.wait_send()

    locals_[1].wait()
    def pick_left(k, carry):
        for t in range(terms):
            picked[t * blocks + k] = left[t, left_ids[k]] * (sources[t, k] >= 0).astype(F32)
        return carry

    lax.fori_loop(0, blocks, pick_left, 0)

    def split_left(n, carry):
        high, low = split(picked[n])
        left_split[n, :tile] = high
        left_split[n, tile:] = low
        return carry

    lax.fori_loop(0, terms * blocks, split_left, 0)
    locals_[2].wait()
    for k in range(blocks):
        inverse[at(k)] = 1.0 / precond[at(k)]
    vector[...] = jnp.zeros_like(vector)
    image[...] = jnp.zeros_like(image)

    zero = jnp.zeros((8, tile), F32)

    def store_search(length):
        def block(k, carry):
            value = search[at(k)] * length
            search[at(k)] = value
            high, low = split(value)
            search_high[k] = high
            search_low[k] = low
            return carry

        lax.fori_loop(0, blocks, block, 0)

    locals_[0].wait()
    spread(site_right, lambda h: seg_copies[h].wait())
    def guess(k, total):
        a_high, a_low = split(site_left[k])
        b_high, b_low = split(site_right[at(k)])
        value = dot(a_high, b_high) + (dot(a_high, b_low) + dot(a_low, b_high))
        search[at(k)] = value
        return total + folded(value * value)

    store_search(1.0 / jnp.sqrt(total_of(lax.fori_loop(0, blocks, guess, zero)) + EPSILON))

    for t in range(terms):
        seg_copies[parts + t].wait()
    for t in range(terms):

        def pick_right(k, carry):
            picked[k] = right[t, right_ids[k]]
            return carry

        lax.fori_loop(0, blocks, pick_right, 0)

        def split_right(k, carry):
            high, low = split(picked[k].T)
            right_high[k, t * tile:(t + 1) * tile] = high
            right_low[k, t * tile:(t + 1) * tile] = low
            return carry

        lax.fori_loop(0, blocks, split_right, 0)

    def apply_local(low_block, high_block):
        def pick(k, carry):
            for t in range(terms):
                source = jnp.maximum(sources[t, k], 0)
                feed_high[t * blocks + k] = search_high[source]
                feed_low[t * blocks + k] = search_low[source]
            return carry

        lax.fori_loop(low_block, high_block, pick, 0)

        def block(k, carry):
            highs, lows = [], []
            for t in range(terms):
                held = t * blocks + k
                both = dot(left_split[held], feed_high[held])
                inner = both[:tile] + (both[tile:] + dot(left_split[held, :tile], feed_low[held]))
                high, low = split(inner)
                highs.append(high)
                lows.append(low)
            high = jnp.concatenate(highs, axis=1)
            both = dot(jnp.concatenate([high, jnp.concatenate(lows, axis=1)], axis=0), right_high[k])
            part[at(k)] = both[:tile] + (both[tile:] + dot(high, right_low[k]))
            return carry

        lax.fori_loop(low_block, high_block, block, 0)

    def to_partner(h, distance):
        slot = h * places + distance
        return pltpu.make_async_remote_copy(
            src_ref=part.at[rows(h, peer(distance) * 2 + 1 - column)], dst_ref=pair_in.at[slot],
            send_sem=pair_send.at[slot], recv_sem=pair_recv.at[slot],
            device_id={"term": partner}, device_id_type=MESH,
        )

    def along_line(h, distance):
        slot = h * places + distance
        return pltpu.make_async_remote_copy(
            src_ref=line_out.at[slot], dst_ref=line_in.at[slot], send_sem=line_send.at[slot],
            recv_sem=line_recv.at[slot], device_id={"term": peer(distance) * 2 + column},
            device_id_type=MESH,
        )

    order = list(range(1, places)) + [0]

    def apply():
        pairs, lines = [], []
        for h in range(parts):
            apply_local(h * blocks // parts, (h + 1) * blocks // parts)
            pairs.append([to_partner(h, distance) for distance in order])
            for copy in pairs[h]:
                copy.start()
        for h in range(parts):
            lines.append([])
            for distance, copy in zip(order, pairs[h]):
                copy.wait_recv()
                slot = h * places + distance
                line_out[slot] = pair_in[slot] + part[rows(h, peer(distance) * 2 + column)]
                if distance:
                    lines[h].append(along_line(h, distance))
                    lines[h][-1].start()

        def finish(h):
            for copy in lines[h]:
                copy.wait_recv()
            summed = line_out[h * places]
            for distance in range(1, places):
                summed = summed + line_in[h * places + distance]
            search_image[rows(h, me)] = summed

        spread(search_image, finish)
        for h in range(parts):
            for copy in pairs[h] + lines[h]:
                copy.wait_send()

    def step(iteration, energy):
        apply()
        first = iteration == 0
        def measures(k, sums):
            v, i, s, h = vector[at(k)], image[at(k)], search[at(k)], search_image[at(k)]
            return sums[0] + folded(v * h + s * i), sums[1] + folded(s * h)

        cross, own = lax.fori_loop(0, blocks, measures, (zero, zero))
        coupling, curvature = 0.5 * total_of(cross), total_of(own)
        half_gap = 0.5 * (energy - curvature)
        radius = jnp.sqrt(half_gap * half_gap + coupling * coupling)
        keep = jnp.where(
            half_gap >= 0, coupling * coupling / (radius + jnp.abs(half_gap)), radius - half_gap
        )
        norm = jnp.sqrt(keep * keep + coupling * coupling)
        keep, mix = jnp.where(first, 0.0, keep / norm), jnp.where(first, 1.0, -coupling / norm)
        energy = keep * keep * energy + 2.0 * keep * mix * coupling + mix * mix * curvature

        def scale_residual(k, total):
            new_vector = keep * vector[at(k)] + mix * search[at(k)]
            new_image = keep * image[at(k)] + mix * search_image[at(k)]
            vector[at(k)] = new_vector
            image[at(k)] = new_image
            scaled = (new_image - energy * new_vector) * inverse[at(k)]
            search[at(k)] = scaled
            return total + folded(new_vector * scaled)

        projection = total_of(lax.fori_loop(0, blocks, scale_residual, zero))

        def remove(k, total):
            remainder = search[at(k)] - projection * vector[at(k)]
            search[at(k)] = remainder
            return total + folded(remainder * remainder)

        store_search(1.0 / jnp.sqrt(total_of(lax.fori_loop(0, blocks, remove, zero)) + EPSILON))
        return energy

    energy = lax.fori_loop(0, ITERS + 1, step, jnp.zeros((1, 1), F32))
    energy_ref[...] = jnp.broadcast_to(energy, energy_ref.shape)
    scale = math.sqrt(blocks * tile * tile)
    for k in range(blocks):
        if share % 8 == 0:
            out_ref[k] = vector[pl.ds(pl.multiple_of(k * tile + me * share, 8), share)] * scale
        else:
            out_ref[k] = vector[k * tile:(k + 1) * tile] * scale


def shards(
    devices, segs,
    envs_left, envs_right, site_left, site_right, precondition, source_block, left_tile, right_tile,
):
    terms, tiles, tile = envs_left.shape[1], envs_left.shape[2], envs_left.shape[3]
    blocks = site_left.shape[1]
    piece = blocks * tile // devices
    parts = next(n for n in PARTS if blocks % n == 0 and piece % (8 * n) == 0)
    places = devices // 2
    share = tile // devices
    out_rows = share if share % 8 == 0 else tile
    flat = pltpu.VMEM((blocks * tile, tile), F32)
    stack = pltpu.VMEM((blocks, tile, tile), F32)
    slots = pltpu.VMEM((parts * places, piece // parts, tile), F32)
    sems = pltpu.SemaphoreType.DMA((parts * places,))
    hbm = pl.BlockSpec(memory_space=pl.ANY)
    smem = pl.BlockSpec(memory_space=pltpu.SMEM)
    vmem = pl.BlockSpec(memory_space=pltpu.VMEM)
    out, energy = pl.pallas_call(
        functools.partial(kernel, devices, segs, blocks, tile, terms, share, parts),
        out_shape=(
            jax.ShapeDtypeStruct((blocks, out_rows, tile), F32),
            jax.ShapeDtypeStruct((8, 128), F32),
        ),
        in_specs=[hbm] * 5 + [smem] * 3,
        out_specs=(vmem, vmem),
        scratch_shapes=[
            pltpu.VMEM((terms, tiles, tile, tile), F32),
            pltpu.VMEM((terms, tiles, tile, tile), F32),
            stack,
            flat,
            flat,
            pltpu.VMEM((terms * blocks, 2 * tile, tile), BF16),
            pltpu.VMEM((blocks, terms * tile, tile), BF16),
            pltpu.VMEM((blocks, terms * tile, tile), BF16),
            pltpu.VMEM((blocks, tile, tile), BF16),
            pltpu.VMEM((blocks, tile, tile), BF16),
            pltpu.VMEM((terms * blocks, tile, tile), F32),
            pltpu.VMEM((terms * blocks, tile, tile), BF16),
            pltpu.VMEM((terms * blocks, tile, tile), BF16),
            flat, flat, flat, flat, flat, flat,
            slots, slots, slots,
            pltpu.SemaphoreType.DMA((3,)),
            pltpu.SemaphoreType.DMA((parts + terms,)),
            pltpu.SemaphoreType.DMA((parts + terms,)),
            sems, sems, sems, sems, sems, sems, sems, sems,
        ],
        compiler_params=pltpu.CompilerParams(
            collective_id=0, has_side_effects=True
        ),
    )(
        envs_left[0], envs_right[0], site_left[0], site_right[0].reshape(blocks * tile, tile), precondition.reshape(blocks * tile, tile),
        source_block[0], left_tile[0], right_tile[0],
    )
    if out_rows != share:
        out = lax.dynamic_slice_in_dim(out, lax.axis_index("term") * share, share, 1)
    return (out.reshape(1, blocks, share * tile), energy[0, :1])


def solution(mesh):
    in_specs = (
        P("seg", "term", None, None, None),
        P("seg", "term", None, None, None),
        P("seg", None, None, None),
        P("seg", None, None, None),
        P("seg", None, None),
        P("seg", "term", None),
        P("seg", None),
        P("seg", None),
    )
    out_specs = (P("seg", None, "term"), P("seg"))
    body = functools.partial(shards, mesh.shape["term"], mesh.shape["seg"])
    return jax.shard_map(body, mesh=mesh, in_specs=in_specs, out_specs=out_specs, check_vma=False)
```
